32 devices in a mesh: tm: 4 (over y, core), space: 8 (over z, x).
Axes of the slice: x: 2, y: 2, z: 4, core: 2. Of those that a mesh axis runs over, the one named last changes fastest.
Arguments:
- query_rows: bfloat16 [8192, 2560], P(('tm', 'space')), may hold values from -18 to 18
- key_rows: bfloat16 [8192, 2560], P(('tm', 'space')), may hold values from -7 to 7
- value_rows: bfloat16 [8192, 2560], P(('tm', 'space')), may hold values from -12 to 12
- out_cotangent: bfloat16 [8192, 2560], P(('tm', 'space')), may hold values from -12 to 12
- tile_slot: int32 [8192], P(('tm', 'space')), may hold values from 0 to 8191, as said below
- window_reach: int32 [4, 8, 2], P(None, 'space'), may hold values from 0 to 1, as said below
Outputs:
- attended: bfloat16 [8192, 2560], P(('tm', 'space'))
- query_grad: bfloat16 [8192, 2560], P(('tm', 'space'))
- key_grad: bfloat16 [8192, 2560], P(('tm', 'space'))
- value_grad: bfloat16 [8192, 2560], P(('tm', 'space'))
The draws below stay inside these ranges and needn't reach their ends.
Inputs may be any that keep to these rules, and one draw needn't show every extreme that they name: `tile_slot`: A permutation of the tile-order positions. The raster tokens r * 256 to r * 256 + 256 - 1 (shard r, counted over tm first, then space) take, for every shard d, exactly the 8 positions d * 256 + r * 8 to d * 256 + r * 8 + 7. `window_reach`: entry 0 is 0 in the lowest slab and entry 1 is 0 in the highest slab.
All inputs are finite; a program needn't handle non-finite values.
Results may differ from the reference program's by a relative error of at most 0.0053.
Values may be sent and summed in bfloat16 or wider, within the bound.
A program may use at most 192 MiB of HBM per device.

```python
import jax
import jax.numpy as jnp
from jax import lax

H = 20
HD = 128
TILE = 256
TILES_DEV = 1
TOK_DEV = 256
TOKENS = 8192
N_TM = 4
N_SPACE = 8


def balanced_slots(seed_key):
    shard_count = N_TM * N_SPACE
    per_peer = TOK_DEV // shard_count
    shard_keys = jax.random.split(seed_key, shard_count)

    def one_shard(shard_key, shard_index):
        shuffled = jax.random.permutation(shard_key, TOK_DEV)
        inverse = jnp.argsort(shuffled).astype(jnp.int32)
        return inverse // per_peer * TOK_DEV + shard_index * per_peer + inverse % per_peer
    slots = jax.vmap(one_shard)(shard_keys, jnp.arange(shard_count, dtype=jnp.int32))
    return slots.reshape(-1).astype(jnp.int32)


def draw_tile_slot(key, part):
    return balanced_slots(jax.random.fold_in(key, 11))


def draw_window_reach(key, part):
    columns = N_SPACE * TILES_DEV
    coin_flips = (jax.random.randint(jax.random.fold_in(key, 23), (N_TM, columns, 2), 0, 4) > 0).astype(jnp.int32)
    slab_index = jnp.arange(N_TM)[:, None, None]
    which_side = jnp.arange(2)[None, None, :]
    border = (slab_index == 0) & (which_side == 0) | (slab_index == N_TM - 1) & (which_side == 1)
    return jnp.where(border, 0, coin_flips).astype(jnp.int32)


def draw_query_rows(key, part):
    drawn = 1.5 * jnp.clip(jax.random.normal(jax.random.fold_in(key, 31), (TOKENS, H * HD), jnp.float32), -6.0, 6.0)
    return drawn.astype(jnp.bfloat16)


def draw_key_rows(key, part):
    drawn = jnp.clip(jax.random.normal(jax.random.fold_in(key, 41), (TOKENS, H * HD), jnp.float32), -6.0, 6.0)
    return drawn.astype(jnp.bfloat16)


def block_levels(key, shape, cuts, smallest, top_value):
    loudness = 1.0
    for dim, blocks in cuts:
        heights = jax.random.uniform(jax.random.fold_in(jax.random.fold_in(key, 6), dim), (blocks,), jnp.float32, smallest / len(cuts), top_value / len(cuts))
        loudness = loudness * jnp.repeat(jnp.exp(heights), shape[dim] // blocks).reshape((-1,) + (1,) * (len(shape) - 1 - dim))
    return loudness


def bell_draw(stream_key, shape, scale, limit, pieces=(), kind=jnp.bfloat16):
    entries = scale * jax.random.normal(stream_key, shape, jnp.float32)
    if pieces:
        entries = entries * block_levels(stream_key, shape, pieces, -0.22, 0.18)
    return jnp.clip(entries, -limit, limit).astype(kind)


def setup_inputs(seed: int = 0) -> dict:
    seeds = jax.random.split(jax.random.key(seed), 7)
    return {
        "query_rows": draw_query_rows(jax.random.fold_in(seeds[6], 71), 0),
        "key_rows": draw_key_rows(jax.random.fold_in(seeds[6], 71), 0),
        "value_rows": bell_draw(seeds[2], (TOKENS, H * HD), 2.0, 12.0, ((0, 32),)),
        "out_cotangent": bell_draw(seeds[3], (TOKENS, H * HD), 2.0, 12.0, ((0, 32),)),
        "tile_slot": draw_tile_slot(jax.random.fold_in(seeds[6], 71), 0),
        "window_reach": draw_window_reach(jax.random.fold_in(seeds[6], 71), 0),
    }


def rounded(values):
    return lax.optimization_barrier(values.astype(jnp.bfloat16)).astype(jnp.float32)


def pick_five(piece):
    return jnp.stack([piece[0, 1], piece[1, 1], piece[2, 1], piece[1, 0], piece[1, 2]])


def start_of(*values):
    return tuple(jnp.asarray(value).astype(jnp.int32) for value in values)


def reference(query_rows, key_rows, value_rows, out_cotangent, tile_slot, window_reach):
    softmax_scale = HD ** -0.5
    columns = N_SPACE * TILES_DEV
    tile_count = N_TM * columns
    source_of = jnp.zeros((TOKENS,), jnp.int32).at[tile_slot].set(jnp.arange(TOKENS, dtype=jnp.int32))

    def tiled(array):
        shaped = array[source_of].reshape(N_TM, columns, TILE, H, HD)
        return jnp.pad(shaped, ((1, 1), (1, 1), (0, 0), (0, 0), (0, 0)))

    query_pad = tiled(query_rows)
    key_pad = tiled(key_rows)
    value_pad = tiled(value_rows)
    grad_pad = tiled(out_cotangent)
    border = jnp.zeros((1, columns, 2), jnp.int32)
    reach_pad = jnp.concatenate([border, window_reach.astype(jnp.int32), border], axis=0)

    def take_five(array, slab_index, column):
        piece = lax.dynamic_slice(array, start_of(slab_index, column, 0, 0, 0), (3, 3, TILE, H, HD))
        return pick_five(piece).astype(jnp.float32)

    def take_own(array, slab_index, column):
        piece = lax.dynamic_slice(array, start_of(slab_index + 1, column + 1, 0, 0, 0), (1, 1, TILE, H, HD))
        return piece[0, 0].astype(jnp.float32)

    def forward_tile(tile_index):
        slab_index = (tile_index // columns).astype(jnp.int32)
        column = (tile_index % columns).astype(jnp.int32)
        keys_near = take_five(key_pad, slab_index, column)
        values_near = take_five(value_pad, slab_index, column)
        queries = take_own(query_pad, slab_index, column)
        cotangent = take_own(grad_pad, slab_index, column)
        reach_here = lax.dynamic_slice(reach_pad, start_of(slab_index + 1, column, 0), (1, 1, 2))[0, 0]
        allowed = jnp.stack([reach_here[0] > 0, reach_here[0] >= 0, reach_here[1] > 0, column > 0, column < columns - 1])
        visible = allowed[None, None, :, None]
        scores = jnp.einsum('qhd,akhd->hqak', queries, keys_near) * softmax_scale
        row_max = jnp.max(jnp.where(visible, scores, -1e30), axis=(2, 3), keepdims=True)
        expo = jnp.where(visible, jnp.exp(scores - row_max), 0.0)
        row_sum = jnp.sum(expo, axis=(2, 3), keepdims=True)
        weights = expo / row_sum
        weights_low = rounded(weights)
        output = jnp.einsum('hqak,akhd->qhd', weights_low, values_near).astype(jnp.bfloat16)
        dweights = jnp.einsum('qhd,akhd->hqak', cotangent, values_near)
        row_dot = jnp.sum(weights * dweights, axis=(2, 3), keepdims=True)
        dscores = rounded(weights * (dweights - row_dot) * softmax_scale)
        query_part = jnp.einsum('hqak,akhd->qhd', dscores, keys_near).astype(jnp.bfloat16)
        return output, query_part, row_max[:, :, 0, 0], row_sum[:, :, 0, 0], row_dot[:, :, 0, 0]

    outputs, query_parts, maxima, sums, dots = lax.map(forward_tile, jnp.arange(tile_count, dtype=jnp.int32))

    def stat_pad(stat, fill):
        shaped = stat.reshape(N_TM, columns, H, TILE)
        return jnp.pad(shaped, ((1, 1), (1, 1), (0, 0), (0, 0)), constant_values=fill)

    max_pad = stat_pad(maxima, 0.0)
    sum_pad = stat_pad(sums, 1.0)
    dot_pad = stat_pad(dots, 0.0)

    def backward_tile(tile_index):
        slab_index = (tile_index // columns).astype(jnp.int32)
        column = (tile_index % columns).astype(jnp.int32)
        queries = take_five(query_pad, slab_index, column)
        cotangent = take_five(grad_pad, slab_index, column)
        keys_here = take_own(key_pad, slab_index, column)
        values_here = take_own(value_pad, slab_index, column)
        reach_near = lax.dynamic_slice(reach_pad, start_of(slab_index, column, 0), (3, 1, 2))[:, 0]
        included = jnp.stack([reach_near[0, 1] > 0, reach_near[1, 0] >= 0, reach_near[2, 0] > 0, column > 0, column < columns - 1])
        visible = included[:, None, None, None]

        def stat_five(array):
            piece = lax.dynamic_slice(array, start_of(slab_index, column, 0, 0), (3, 3, H, TILE))
            return pick_five(piece)[..., None]

        row_max = stat_five(max_pad)
        row_sum = jnp.where(visible, stat_five(sum_pad), 1.0)
        row_dot = stat_five(dot_pad)
        scores = jnp.einsum('bqhd,khd->bhqk', queries, keys_here) * softmax_scale
        weights = jnp.where(visible, jnp.exp(scores - row_max) / row_sum, 0.0)
        weights_low = rounded(weights)
        dweights = jnp.einsum('bqhd,khd->bhqk', cotangent, values_here)
        dscores = rounded(weights * (dweights - row_dot) * softmax_scale)
        key_part = jnp.einsum('bhqk,bqhd->khd', dscores, queries).astype(jnp.bfloat16)
        value_part = jnp.einsum('bhqk,bqhd->khd', weights_low, cotangent).astype(jnp.bfloat16)
        return key_part, value_part

    key_parts, value_parts = lax.map(backward_tile, jnp.arange(tile_count, dtype=jnp.int32))

    def to_raster(array):
        return array.reshape(TOKENS, H * HD)[tile_slot]

    return (to_raster(outputs), to_raster(query_parts), to_raster(key_parts), to_raster(value_parts))
```

```python
import functools
import math

import jax
import jax.numpy as jnp
from jax import lax
from jax.experimental import pallas as pl
from jax.experimental.pallas import tpu as pltpu
from jax.sharding import PartitionSpec as P

H = 20
HD = 128
TILE = 256
PAIR = 2 * HD
CHUNKS = 2
BOTH = ("tm", "space")
SCALE = HD ** (-0.5)
VMEM_LIMIT = 40 * 1024 * 1024


def device_of(tile, tm_count, space_count):
    if (tm_count, space_count) != (4, 8):
        return tile
    slab, column = tile // 8, tile % 8
    z, core = column // 2, column % 2
    y = slab // 2
    x = (slab + y) % 2
    return (y * 2 + core) * 8 + z * 2 + x


def tile_of(rank, tm_count, space_count):
    if (tm_count, space_count) != (4, 8):
        return rank
    tm, space = rank // 8, rank % 8
    y, core = tm // 2, tm % 2
    z, x = space // 2, space % 2
    return (y * 2 + (x + y) % 2) * 8 + z * 2 + core


def dot(a, b, dims):
    return lax.dot_general(a, b, (dims, ((), ())), preferred_element_type=jnp.float32)


def pack_body(landing_ref, q_ref, k_ref, v_ref, g_ref, kv_ref, qg_ref):
    rows = lax.broadcasted_iota(jnp.int32, (TILE, TILE), 0)
    pick = jnp.where(rows == landing_ref[...], 1.0, 0.0).astype(jnp.bfloat16)
    for ref, out, at in ((k_ref, kv_ref, 0), (v_ref, kv_ref, 1), (q_ref, qg_ref, 0), (g_ref, qg_ref, 1)):
        moved = dot(pick, ref[...], ((1,), (0,)))
        out[:, at * PAIR : (at + 1) * PAIR] = moved.astype(jnp.bfloat16)


def pack(landing, arrays, chunk, steps):
    width = steps * 2 * PAIR
    rows = arrays[0].shape[0]
    source = pl.BlockSpec((rows, PAIR), lambda i: (0, chunk * steps + i))
    target = pl.BlockSpec((rows, 2 * PAIR), lambda i: (0, i))
    shape = jax.ShapeDtypeStruct((rows, width), jnp.bfloat16)
    return pl.pallas_call(
        pack_body,
        grid=(steps,),
        in_specs=[pl.BlockSpec((1, rows), lambda i: (0, 0))] + [source] * 4,
        out_specs=[target] * 2,
        out_shape=[shape] * 2,
        cost_estimate=pl.CostEstimate(
            flops=4 * rows * rows * width, bytes_accessed=8 * rows * width, transcendentals=0
        ),
        name="pack",
    )(landing[None, :], *arrays)


def unpack_body(steps, landing_ref, *refs):
    chunk_refs, (first_ref, second_ref) = refs[:-2], refs[-2:]
    columns = lax.broadcasted_iota(jnp.int32, (TILE, TILE), 1)
    pick = jnp.where(columns == landing_ref[...], 1.0, 0.0).astype(jnp.bfloat16)
    step = pl.program_id(0)
    for chunk, ref in enumerate(chunk_refs):

        @pl.when(step // steps == chunk)
        def _(ref=ref):
            moved = dot(pick, ref[...], ((1,), (0,))).astype(jnp.bfloat16)
            first_ref[...] = moved[:, :PAIR]
            second_ref[...] = moved[:, PAIR:]


def unpack(landing, chunks, steps):
    rows = chunks[0].shape[0]
    total = steps * len(chunks)
    specs = [
        pl.BlockSpec(
            (rows, 2 * PAIR), lambda i, c=c: (0, jnp.clip(i - c * steps, 0, steps - 1))
        )
        for c in range(len(chunks))
    ]
    shape = jax.ShapeDtypeStruct((rows, total * PAIR), jnp.bfloat16)
    return pl.pallas_call(
        functools.partial(unpack_body, steps),
        grid=(total,),
        in_specs=[pl.BlockSpec((rows, 1), lambda i: (0, 0))] + specs,
        out_specs=[pl.BlockSpec((rows, PAIR), lambda i: (0, i))] * 2,
        out_shape=[shape] * 2,
        cost_estimate=pl.CostEstimate(
            flops=4 * rows * rows * total * PAIR,
            bytes_accessed=8 * rows * total * PAIR,
            transcendentals=0,
        ),
        name="unpack",
    )(landing[:, None], *chunks)


def attend_body(bias_ref, qg_ref, *refs):
    kv_refs, od_ref, own_ref, side_refs = refs[:5], refs[5], refs[6], refs[7:]
    to_log2 = SCALE * math.log2(math.e)
    for head in range(2):
        low = pl.ds(head * HD, HD)
        high = pl.ds(PAIR + head * HD, HD)
        queries, cotangent = qg_ref[:, low], qg_ref[:, high]
        scores = []
        for near, kv in enumerate(kv_refs):
            block = dot(kv[:, low], queries, ((1,), (1,))) * to_log2
            scores.append(block if near == 0 else block + bias_ref[near - 1])
        row_max = functools.reduce(
            jnp.maximum, [jnp.max(block, axis=0, keepdims=True) for block in scores]
        )
        expo = [jnp.exp2(block - row_max) for block in scores]
        row_sum = sum(jnp.sum(block, axis=0, keepdims=True) for block in expo)
        inverse = 1.0 / row_sum
        weights = [block * inverse for block in expo]
        dweights = [dot(kv[:, high], cotangent, ((1,), (1,))) for kv in kv_refs]
        row_dot = sum(
            jnp.sum(w * d, axis=0, keepdims=True) for w, d in zip(weights, dweights)
        )
        output = jnp.zeros((HD, TILE), jnp.float32)
        query_part = jnp.zeros((HD, TILE), jnp.float32)
        for near, kv in enumerate(kv_refs):
            weights_low = weights[near].astype(jnp.bfloat16)
            dscores = (weights[near] * (dweights[near] - row_dot)).astype(jnp.bfloat16)
            output += dot(kv[:, high], weights_low, ((0,), (0,)))
            query_part += dot(kv[:, low], dscores, ((0,), (0,)))
            key_term = dot(dscores, queries, ((1,), (0,))) * SCALE
            value_term = dot(weights_low, cotangent, ((1,), (0,)))
            target = own_ref if near == 0 else side_refs[near - 1]
            target[:, low] = key_term.astype(target.dtype)
            target[:, high] = value_term.astype(target.dtype)
        od_ref[:, low] = output.T.astype(jnp.bfloat16)
        od_ref[:, high] = (query_part * SCALE).T.astype(jnp.bfloat16)


def attend(bias, qg, kvs, steps):
    rows, width = qg.shape
    block = pl.BlockSpec((rows, 2 * PAIR), lambda i: (0, i))
    low = jax.ShapeDtypeStruct((rows, width), jnp.bfloat16)
    full = jax.ShapeDtypeStruct((rows, width), jnp.float32)
    heads = steps * 2
    return pl.pallas_call(
        attend_body,
        grid=(steps,),
        in_specs=[pl.BlockSpec(memory_space=pltpu.SMEM)] + [block] * 6,
        out_specs=[block] * 6,
        out_shape=[low, full, low, low, low, low],
        compiler_params=pltpu.CompilerParams(vmem_limit_bytes=VMEM_LIMIT),
        cost_estimate=pl.CostEstimate(
            flops=3 * heads * 6 * 5 * 2 * rows * rows * HD,
            bytes_accessed=13 * rows * width * 2,
            transcendentals=heads * 5 * rows * rows,
        ),
        name="attend",
    )(bias, qg, *kvs)


def shards(query_rows, key_rows, value_rows, out_cotangent, tile_slot, window_reach):
    tokens_here, channels = query_rows.shape
    tm_count = lax.axis_size("tm")
    space_count = lax.axis_size("space")
    device_count = tm_count * space_count
    per_peer = tokens_here // device_count
    slab, space = lax.axis_index("tm"), lax.axis_index("space")
    rank = slab * space_count + space
    steps = channels // PAIR // CHUNKS
    owner = functools.partial(device_of, tm_count=tm_count, space_count=space_count)

    def passed(block, slab_move, column_move):
        pairs = []
        for tile in range(device_count):
            to_slab = tile // space_count + slab_move
            to_column = tile % space_count + column_move
            if 0 <= to_slab < tm_count and 0 <= to_column < space_count:
                pairs.append((owner(tile), owner(to_slab * space_count + to_column)))
        return lax.ppermute(block, BOTH, pairs)

    landing = owner(tile_slot // tokens_here) * per_peer + tile_slot % tokens_here - rank * per_peer

    reach = lax.dynamic_index_in_dim(window_reach, slab, 0, keepdims=False)[0]
    reach = lax.ppermute(reach, BOTH, [(tile, owner(tile)) for tile in range(device_count)])
    column = tile_of(rank, tm_count, space_count) % space_count
    open_sides = jnp.stack([reach[0] > 0, reach[1] > 0, column > 0, column < space_count - 1])
    bias = jnp.where(open_sides, 0.0, -1e30).astype(jnp.float32)

    def exchange(rows):
        return lax.all_to_all(rows, BOTH, split_axis=0, concat_axis=0, tiled=True)

    moves = ((1, 0), (-1, 0), (0, 1), (0, -1))
    arrays = (query_rows, key_rows, value_rows, out_cotangent)
    back_outputs, back_terms = [], []
    for chunk in range(CHUNKS):
        send_kv, send_qg = pack(landing, arrays, chunk, steps)
        kv = exchange(send_kv)
        qg = exchange(send_qg)
        kvs = [kv] + [passed(kv, *move) for move in moves]
        outputs, own, *sides = attend(bias, qg, kvs, steps)
        back_outputs.append(exchange(outputs))
        terms = [passed(side, -a, -b) for side, (a, b) in zip(sides, moves)]
        total = own + sum(term.astype(jnp.float32) for term in terms)
        back_terms.append(exchange(total.astype(jnp.bfloat16)))
    attended, query_grad = unpack(landing, back_outputs, steps)
    key_grad, value_grad = unpack(landing, back_terms, steps)
    return (attended, query_grad, key_grad, value_grad)


def solution(mesh):
    rows = P(BOTH, None)
    return jax.shard_map(
        shards,
        mesh=mesh,
        in_specs=(rows, rows, rows, rows, P(BOTH), P(None, "space", None)),
        out_specs=(rows, rows, rows, rows),
        check_vma=False,
    )
```

```python
import functools
import math

import jax
import jax.numpy as jnp
from jax import lax
from jax.experimental import pallas as pl
from jax.experimental.pallas import tpu as pltpu
from jax.sharding import PartitionSpec as P

H = 20
HD = 128
TILE = 256
PAIR = 2 * HD
CHUNKS = 2
BOTH = ("tm", "space")
SCALE = HD ** (-0.5)
VMEM_LIMIT = 60 * 1024 * 1024


def device_of(tile, tm_count, space_count):
    if (tm_count, space_count) != (4, 8):
        return tile
    slab, column = tile // 8, tile % 8
    z, core = column // 2, column % 2
    y = slab // 2
    x = (slab + y) % 2
    return (y * 2 + core) * 8 + z * 2 + x


def tile_of(rank, tm_count, space_count):
    if (tm_count, space_count) != (4, 8):
        return rank
    tm, space = rank // 8, rank % 8
    y, core = tm // 2, tm % 2
    z, x = space // 2, space % 2
    return (y * 2 + (x + y) % 2) * 8 + z * 2 + core


def dot(a, b, dims):
    return lax.dot_general(a, b, (dims, ((), ())), preferred_element_type=jnp.float32)


def pack_body(landing_ref, first_ref, second_ref, *refs):
    out_ref = refs[-1]
    rows = lax.broadcasted_iota(jnp.int32, (TILE, TILE), 0)
    pick = jnp.where(rows == landing_ref[...], 1.0, 0.0).astype(jnp.bfloat16)
    for at, ref in enumerate((first_ref, second_ref)):
        moved = dot(pick, ref[...], ((1,), (0,)))
        out_ref[:, at * PAIR : (at + 1) * PAIR] = moved.astype(jnp.bfloat16)


def pack(landing, first, second, chunk, steps, after=()):
    width = steps * 2 * PAIR
    rows = first.shape[0]
    source = pl.BlockSpec((rows, PAIR), lambda i: (0, chunk * steps + i))
    return pl.pallas_call(
        pack_body,
        grid=(steps,),
        in_specs=[pl.BlockSpec((1, rows), lambda i: (0, 0)), source, source]
        + [pl.BlockSpec(memory_space=pl.ANY)] * len(after),
        out_specs=pl.BlockSpec((rows, 2 * PAIR), lambda i: (0, i)),
        out_shape=jax.ShapeDtypeStruct((rows, width), jnp.bfloat16),
        compiler_params=pltpu.CompilerParams(vmem_limit_bytes=VMEM_LIMIT),
        cost_estimate=pl.CostEstimate(
            flops=2 * rows * rows * width, bytes_accessed=4 * rows * width, transcendentals=0
        ),
        name="pack",
    )(landing[None, :], first, second, *after)


def unpack_body(landing_ref, moved_ref, *refs):
    first_ref, second_ref = refs[-2:]
    columns = lax.broadcasted_iota(jnp.int32, (TILE, TILE), 1)
    pick = jnp.where(columns == landing_ref[...], 1.0, 0.0).astype(jnp.bfloat16)
    moved = dot(pick, moved_ref[...], ((1,), (0,))).astype(jnp.bfloat16)
    first_ref[...] = moved[:, :PAIR]
    second_ref[...] = moved[:, PAIR:]


def unpack(landing, moved, before, chunk, steps):
    rows = moved.shape[0]
    shape = jax.ShapeDtypeStruct((rows, CHUNKS * steps * PAIR), jnp.bfloat16)
    return pl.pallas_call(
        unpack_body,
        grid=(steps,),
        in_specs=[
            pl.BlockSpec((rows, 1), lambda i: (0, 0)),
            pl.BlockSpec((rows, 2 * PAIR), lambda i: (0, i)),
        ]
        + [pl.BlockSpec(memory_space=pl.ANY)] * len(before),
        out_specs=[pl.BlockSpec((rows, PAIR), lambda i: (0, chunk * steps + i))] * 2,
        out_shape=[shape] * 2,
        input_output_aliases={2 + i: i for i in range(len(before))},
        compiler_params=pltpu.CompilerParams(vmem_limit_bytes=VMEM_LIMIT),
        cost_estimate=pl.CostEstimate(
            flops=4 * rows * rows * steps * PAIR,
            bytes_accessed=8 * rows * steps * PAIR,
            transcendentals=0,
        ),
        name="unpack",
    )(landing[:, None], moved, *before)


def attend_body(bias_ref, qg_ref, *refs):
    kv_refs, od_ref, own_ref, side_refs = refs[:5], refs[5], refs[6], refs[7:]
    to_log2 = SCALE * math.log2(math.e)
    for head in range(2):
        low = pl.ds(head * HD, HD)
        high = pl.ds(PAIR + head * HD, HD)
        queries, cotangent = qg_ref[:, low], qg_ref[:, high]
        scores = []
        for near, kv in enumerate(kv_refs):
            block = dot(kv[:, low], queries, ((1,), (1,))) * to_log2
            scores.append(block if near == 0 else block + bias_ref[near - 1])
        row_max = functools.reduce(
            jnp.maximum, [jnp.max(block, axis=0, keepdims=True) for block in scores]
        )
        expo = [jnp.exp2(block - row_max) for block in scores]
        row_sum = sum(jnp.sum(block, axis=0, keepdims=True) for block in expo)
        inverse = 1.0 / row_sum
        weights = [block * inverse for block in expo]
        dweights = [dot(kv[:, high], cotangent, ((1,), (1,))) for kv in kv_refs]
        row_dot = sum(
            jnp.sum(w * d, axis=0, keepdims=True) for w, d in zip(weights, dweights)
        )
        output = jnp.zeros((HD, TILE), jnp.float32)
        query_part = jnp.zeros((HD, TILE), jnp.float32)
        for near, kv in enumerate(kv_refs):
            weights_low = weights[near].astype(jnp.bfloat16)
            dscores = (weights[near] * (dweights[near] - row_dot)).astype(jnp.bfloat16)
            output += dot(kv[:, high], weights_low, ((0,), (0,)))
            query_part += dot(kv[:, low], dscores, ((0,), (0,)))
            key_term = dot(dscores, queries, ((1,), (0,))) * SCALE
            value_term = dot(weights_low, cotangent, ((1,), (0,)))
            target = own_ref if near == 0 else side_refs[near - 1]
            target[:, low] = key_term.astype(target.dtype)
            target[:, high] = value_term.astype(target.dtype)
        od_ref[:, low] = output.T.astype(jnp.bfloat16)
        od_ref[:, high] = (query_part * SCALE).T.astype(jnp.bfloat16)


def attend(bias, qg, kvs, steps):
    rows, width = qg.shape
    block = pl.BlockSpec((rows, 2 * PAIR), lambda i: (0, i))
    low = jax.ShapeDtypeStruct((rows, width), jnp.bfloat16)
    full = jax.ShapeDtypeStruct((rows, width), jnp.float32)
    heads = steps * 2
    return pl.pallas_call(
        attend_body,
        grid=(steps,),
        in_specs=[pl.BlockSpec(memory_space=pltpu.SMEM)] + [block] * 6,
        out_specs=[block] * 6,
        out_shape=[low, full, low, low, low, low],
        compiler_params=pltpu.CompilerParams(vmem_limit_bytes=VMEM_LIMIT),
        cost_estimate=pl.CostEstimate(
            flops=3 * heads * 6 * 5 * 2 * rows * rows * HD,
            bytes_accessed=13 * rows * width * 2,
            transcendentals=heads * 5 * rows * rows,
        ),
        name="attend",
    )(bias, qg, *kvs)


def shards(query_rows, key_rows, value_rows, out_cotangent, tile_slot, window_reach):
    tokens_here, channels = query_rows.shape
    tm_count = lax.axis_size("tm")
    space_count = lax.axis_size("space")
    device_count = tm_count * space_count
    per_peer = tokens_here // device_count
    slab, space = lax.axis_index("tm"), lax.axis_index("space")
    rank = slab * space_count + space
    steps = channels // PAIR // CHUNKS
    owner = functools.partial(device_of, tm_count=tm_count, space_count=space_count)

    def passed(block, slab_move, column_move):
        pairs = []
        for tile in range(device_count):
            to_slab = tile // space_count + slab_move
            to_column = tile % space_count + column_move
            if 0 <= to_slab < tm_count and 0 <= to_column < space_count:
                pairs.append((owner(tile), owner(to_slab * space_count + to_column)))
        return lax.ppermute(block, BOTH, pairs)

    landing = owner(tile_slot // tokens_here) * per_peer + tile_slot % tokens_here - rank * per_peer

    reach = lax.dynamic_index_in_dim(window_reach, slab, 0, keepdims=False)[0]
    reach = lax.ppermute(reach, BOTH, [(tile, owner(tile)) for tile in range(device_count)])
    column = tile_of(rank, tm_count, space_count) % space_count
    open_sides = jnp.stack([reach[0] > 0, reach[1] > 0, column > 0, column < space_count - 1])
    bias = jnp.where(open_sides, 0.0, -1e30).astype(jnp.float32)

    def exchange(rows):
        return lax.all_to_all(rows, BOTH, split_axis=0, concat_axis=0, tiled=True)

    moves = ((1, 0), (-1, 0), (0, 1), (0, -1))
    back_outputs, back_terms = [], []
    for chunk in range(CHUNKS):
        kv = exchange(pack(landing, key_rows, value_rows, chunk, steps))
        qg = exchange(pack(landing, query_rows, out_cotangent, chunk, steps))
        kvs = [kv] + [passed(kv, *move) for move in moves]
        outputs, own, *sides = attend(bias, qg, kvs, steps)
        back_outputs.append(exchange(outputs))
        terms = [passed(side, -a, -b) for side, (a, b) in zip(sides, moves)]
        total = own + sum(term.astype(jnp.float32) for term in terms)
        back_terms.append(exchange(total.astype(jnp.bfloat16)))
    output_pair, term_pair = (), ()
    for chunk in range(CHUNKS):
        output_pair = unpack(landing, back_outputs[chunk], output_pair, chunk, steps)
        term_pair = unpack(landing, back_terms[chunk], term_pair, chunk, steps)
    return (*output_pair, *term_pair)


def solution(mesh):
    rows = P(BOTH, None)
    return jax.shard_map(
        shards,
        mesh=mesh,
        in_specs=(rows, rows, rows, rows, P(BOTH), P(None, "space", None)),
        out_specs=(rows, rows, rows, rows),
        check_vma=False,
    )
```
